32 devices in a mesh: dp: 8 (over z, y), mp: 4 (over x, core).
Axes of the slice: x: 2, y: 2, z: 4, core: 2. Of those that a mesh axis runs over, the one named last changes fastest.
Arguments:
- query_states: bfloat16 [64, 32, 768], P('dp', None, 'mp'), may hold values from -6 to 6
- passage_states: bfloat16 [1024, 768, 128], P('dp', 'mp'), may hold values from -6 to 6
- projection: bfloat16 [768, 128], P('mp'), may hold values from -0.21875 to 0.21875
- candidates: int32 [64, 64], P(('dp', 'mp')), may hold values from 0 to 1023, as said below
Outputs:
- losses: float32 [64], P(('dp', 'mp'))
- weight_grad: float32 [768, 128], P('mp')
- query_grads: float32 [64, 32, 768], P('dp', None, 'mp')
- passage_grads: float32 [1024, 768, 128], P('dp', 'mp')
The draws below stay inside these ranges and needn't reach their ends.
Inputs may be any that keep to these rules, and one draw needn't show every extreme that they name: `candidates`: the passage with id p is held by owner p // 32. Among the 128 entries of the 2 queries of one owner, at most 8 name passages of any one owner; in every draw some owners receive exactly 8 entries from every owner. A passage may be listed more than once, by one query or by several.
All inputs are finite; a program needn't handle non-finite values.
Results may differ from the reference program's by a relative error of at most 0.0064.
Values may be sent and summed in bfloat16 or wider, within the bound.
A program may use at most 192 MiB of HBM per device.

```python
import jax
import jax.numpy as jnp
from jax import lax

H = 768
E = 128
LQ = 32
LP = 128
K = 64
QL = 2
PL = 32
OWNERS = 32
CAP = 8
QUERIES = 64
PASSAGES = 1024


def draw_candidates(key, part):
    hot_key, rest_key = jax.random.split(key)
    order = jax.random.permutation(hot_key, jnp.arange(OWNERS, dtype=jnp.int32))
    hot_owners = order[:OWNERS // 4]
    cold_owners = order[OWNERS // 4:]

    def one_source(source):
        source_key = jax.random.fold_in(rest_key, source)
        pick_key, local_key, mix_key = jax.random.split(source_key, 3)
        picked = jax.random.permutation(pick_key, cold_owners)[:OWNERS // 4]
        chosen = jnp.concatenate([hot_owners, picked])
        owner_list = jnp.repeat(chosen, CAP, total_repeat_length=QL * K)
        local_list = jax.random.randint(local_key, (QL * K,), 0, PL, dtype=jnp.int32)
        id_list = owner_list * PL + local_list
        id_list = jax.random.permutation(mix_key, id_list)
        return id_list.reshape(QL, K)
    sources = jnp.arange(OWNERS, dtype=jnp.int32)
    return jax.vmap(one_source)(sources).reshape(QL * OWNERS, K).astype(jnp.int32)


def levels(own_key, extent, cuts, smallest, largest):
    factor_of = 1.0
    for position, blocks in cuts:
        draws = jax.random.uniform(jax.random.fold_in(jax.random.fold_in(own_key, 6), position), (blocks,), jnp.float32, smallest / len(cuts), largest / len(cuts))
        factor_of = factor_of * jnp.repeat(jnp.exp(draws), extent[position] // blocks).reshape((-1,) + (1,) * (len(extent) - 1 - position))
    return factor_of


def gaussian(rng, extent, deviation, reach, shards=(), kind=jnp.bfloat16):
    array = deviation * jax.random.normal(rng, extent, jnp.float32)
    if shards:
        array = array * levels(rng, extent, shards, -0.22, 0.18)
    return jnp.clip(array, -reach, reach).astype(kind)


def setup_inputs(seed: int = 0) -> dict:
    streams_of = jax.random.split(jax.random.key(seed), 5)
    query_states = gaussian(streams_of[0], (QUERIES, LQ, H), 1.0, 6.0, ((0, 8), (2, 4)))
    passage_states = gaussian(streams_of[1], (PASSAGES, H, LP), 1.0, 6.0, ((0, 8), (1, 4)))
    projection = gaussian(streams_of[2], (H, E), H ** -0.5, 0.21875, ((0, 4),))
    candidates = draw_candidates(jax.random.fold_in(streams_of[4], 71), 0)
    return dict(query_states=query_states, passage_states=passage_states, projection=projection, candidates=candidates)


sharpness = 10.0
norm_eps = 1e-06

def unit_rows(pre):
    norm = jnp.sqrt(lax.optimization_barrier(jnp.sum(pre * pre, axis=-1, keepdims=True)) + norm_eps)
    return (pre / norm, norm)

def unit_back(grad, unit, norm):
    inner = lax.optimization_barrier(jnp.sum(grad * unit, axis=-1, keepdims=True))
    return ((grad - unit * inner) / norm).astype(jnp.bfloat16)

def soft_maxsim(sim):
    expo = jnp.exp(sharpness * sim)
    total = lax.optimization_barrier(jnp.sum(expo, axis=-1, keepdims=True))
    weights = expo / total
    score = lax.optimization_barrier(jnp.sum(jnp.log(total[..., 0]), axis=-1)) / sharpness
    return (score, weights)

def loss_parts(scores):
    expo = jnp.exp(scores)
    total = lax.optimization_barrier(jnp.sum(expo, axis=-1, keepdims=True))
    prob = expo / total
    losses = jnp.log(total[..., 0]) - scores[..., 0]
    score_grad = prob.at[..., 0].add(-1.0)
    return (losses, score_grad)

def reference(query_states, passage_states, projection, candidates):
    f32 = jnp.float32
    width = projection.shape[1]
    passage_rows_all = jnp.transpose(passage_states, (0, 2, 1)).reshape(-1, H)
    query_pre = jnp.dot(query_states.reshape(-1, H), projection, preferred_element_type=f32)
    passage_pre = jnp.dot(passage_rows_all, projection, preferred_element_type=f32)
    query_unit, query_norm = unit_rows(query_pre)
    passage_unit, passage_norm = unit_rows(passage_pre)
    query_emb = query_unit.astype(jnp.bfloat16).reshape(QUERIES, LQ, width)
    passage_emb = passage_unit.astype(jnp.bfloat16).reshape(PASSAGES, LP, width)

    def one_query(carry, inputs):
        query_one, listed = inputs
        fetched = passage_emb[listed].astype(f32)
        query_f = query_one.astype(f32)
        sim = jnp.einsum('ie,kje->kij', query_f, fetched, precision=lax.Precision.HIGHEST)
        scores, weights = soft_maxsim(sim)
        loss_one, score_grad = loss_parts(scores)
        sim_grad = (score_grad[:, None, None] * weights).astype(jnp.bfloat16).astype(f32)
        query_grad = jnp.einsum('kij,kje->ie', sim_grad, fetched, precision=lax.Precision.HIGHEST)
        passage_term = jnp.einsum('kij,ie->kje', sim_grad, query_f, precision=lax.Precision.HIGHEST)
        carry = carry.at[listed].add(passage_term)
        return (carry, (loss_one, query_grad))
    start_grad = jnp.zeros((PASSAGES, LP, width), f32)
    passage_emb_grad, (losses, query_emb_grad) = lax.scan(one_query, start_grad, (query_emb, candidates))
    query_pre_grad = unit_back(query_emb_grad.reshape(-1, width), query_unit, query_norm)
    passage_pre_grad = unit_back(passage_emb_grad.reshape(-1, width), passage_unit, passage_norm)
    query_grads = jnp.dot(query_pre_grad, projection.T, preferred_element_type=f32)
    passage_grads = jnp.dot(passage_pre_grad, projection.T, preferred_element_type=f32)
    passage_grads = jnp.transpose(passage_grads.reshape(PASSAGES, LP, H), (0, 2, 1))
    weight_grad = jnp.dot(query_states.reshape(-1, H).T, query_pre_grad, preferred_element_type=f32)
    weight_grad = weight_grad + jnp.dot(passage_rows_all.T, passage_pre_grad, preferred_element_type=f32)
    return (losses, weight_grad, query_grads.reshape(QUERIES, LQ, H), passage_grads)
```

```python
import jax
import jax.numpy as jnp
from jax import lax
from jax.experimental import pallas as pl
from jax.experimental.pallas import tpu as pltpu
from jax.sharding import PartitionSpec as P

sharpness = 10.0
norm_eps = 1e-06
BATCH = 8
VMEM_LIMIT = 56 * 1024 * 1024


def unit_rows(pre):
    norm = jnp.sqrt(jnp.sum(pre * pre, axis=-1, keepdims=True) + norm_eps)
    return (pre / norm, norm)


def unit_back(grad, unit, norm):
    inner = jnp.sum(grad * unit, axis=-1, keepdims=True)
    return ((grad - unit * inner) / norm).astype(jnp.bfloat16)


def score_kernel(local_ref, query_ref, pre_ref, visitors_ref, emb_ref, weights_ref, scores_ref):
    def embed(p, carry):
        unit, _ = unit_rows(pre_ref[p])
        emb_ref[p] = unit.astype(jnp.bfloat16)
        return carry

    lax.fori_loop(0, pre_ref.shape[0], embed, 0)

    def slots(b, carry):
        for u in range(BATCH):
            s = b * BATCH + u
            sim = lax.dot_general(
                visitors_ref[query_ref[s]],
                emb_ref[local_ref[s]],
                (((1,), (1,)), ((), ())),
                preferred_element_type=jnp.float32,
            )
            expo = jnp.exp(sharpness * sim)
            total = jnp.sum(expo, axis=-1, keepdims=True)
            weights_ref[s] = expo / total
            score = jnp.sum(jnp.log(total), axis=0, keepdims=True) / sharpness
            scores_ref[s] = jnp.broadcast_to(score, scores_ref.shape[1:])
        return carry

    lax.fori_loop(0, weights_ref.shape[0] // BATCH, slots, 0)


def grad_kernel(
    local_ref, query_ref, grad_ref, pre_ref, emb_ref, visitors_ref, weights_ref,
    query_grad_ref, pre_grad_ref, query_sum, passage_sum
):
    query_sum[...] = jnp.zeros_like(query_sum)
    passage_sum[...] = jnp.zeros_like(passage_sum)

    def slots(b, carry):
        found = []
        for u in range(BATCH):
            s = b * BATCH + u
            p = local_ref[s]
            q = query_ref[s]
            sim_grad = (grad_ref[s] * weights_ref[s]).astype(jnp.bfloat16)
            query_term = jnp.dot(sim_grad, emb_ref[p], preferred_element_type=jnp.float32)
            passage_term = lax.dot_general(
                sim_grad,
                visitors_ref[q],
                (((0,), (0,)), ((), ())),
                preferred_element_type=jnp.float32,
            )
            found.append((p, q, query_term, passage_term))
        for p, q, query_term, passage_term in found:
            query_sum[q] += query_term
            passage_sum[p] += passage_term
        return carry

    lax.fori_loop(0, weights_ref.shape[0] // BATCH, slots, 0)
    query_grad_ref[...] = query_sum[...].astype(jnp.bfloat16)

    def back(p, carry):
        unit, norm = unit_rows(pre_ref[p])
        pre_grad_ref[p] = unit_back(passage_sum[p], unit, norm)
        return carry

    lax.fori_loop(0, pre_ref.shape[0], back, 0)


def swap(array, bit, groups):
    return lax.ppermute(array, "mp", [(i, i ^ bit) for i in range(groups)])


def reduce_mp(states, project, groups, dtype):
    f32 = jnp.float32
    me = lax.axis_index("mp")
    rows = states.shape[0] // groups

    def block(index):
        return project(lax.dynamic_slice_in_dim(states, index * rows, rows, 0))

    if groups != 4:
        return lax.psum_scatter(project(states), "mp", scatter_dimension=0, tiled=True)
    far_out = swap(block(me ^ 3).astype(dtype), 1, groups)
    near_out = swap(block(me ^ 1).astype(dtype), 1, groups)
    far = block(me ^ 2) + far_out.astype(f32)
    far_in = swap(far.astype(dtype), 2, groups)
    return (block(me) + near_out.astype(f32)) + far_in.astype(f32)


def gather_mp(mine, groups):
    if groups != 4:
        return lax.all_gather(mine, "mp", axis=0, tiled=True)
    me = lax.axis_index("mp")
    far = swap(mine, 2, groups)
    near = swap(mine, 1, groups)
    far_near = swap(far, 1, groups)
    odd = (me & 1) == 1
    here = jnp.concatenate([jnp.where(odd, near, mine), jnp.where(odd, mine, near)])
    there = jnp.concatenate([jnp.where(odd, far_near, far), jnp.where(odd, far, far_near)])
    high = (me & 2) == 2
    return jnp.concatenate([jnp.where(high, there, here), jnp.where(high, here, there)])


def exchange(array, axes):
    return lax.all_to_all(array, axes, split_axis=0, concat_axis=0, tiled=True)


def spread(array, axes, size):
    return exchange(jnp.broadcast_to(array[None], (size,) + array.shape), axes)


def on_device(query_states, passage_states, projection, candidates):
    f32 = jnp.float32
    both = ("dp", "mp")
    owners = lax.axis_size(both)
    groups = lax.axis_size("mp")
    replicas = lax.axis_size("dp")
    me = lax.axis_index(both)
    query_rows, listed = candidates.shape
    qry_len = query_states.shape[1]
    emb_dim = projection.shape[1]
    psg_len = passage_states.shape[2]
    passage_rows = passage_states.shape[0] // groups
    requests = query_rows * listed
    capacity = 2 * requests // owners
    slot_total = owners * capacity
    queries = owners * query_rows

    listings = spread(candidates, both, owners).reshape(owners, requests)
    query_pre = reduce_mp(
        query_states,
        lambda s: jnp.einsum("nlh,he->nle", s, projection, preferred_element_type=f32),
        groups,
        f32,
    )
    query_unit, query_norm = unit_rows(query_pre)
    visitors = spread(query_unit.astype(jnp.bfloat16), both, owners)
    visitors = visitors.reshape(queries, qry_len, emb_dim)
    passage_pre = reduce_mp(
        passage_states,
        lambda s: jnp.einsum("nhl,he->nle", s, projection, preferred_element_type=f32),
        groups,
        jnp.bfloat16,
    )

    held = (listings // passage_rows) == me
    within = jnp.cumsum(held.astype(jnp.int32), axis=1) - 1
    chosen = held[:, None, :] & (
        within[:, None, :] == jnp.arange(capacity, dtype=jnp.int32)[None, :, None]
    )
    entry = jnp.arange(requests, dtype=jnp.int32)
    valid = jnp.any(chosen, axis=-1).reshape(-1)
    entry_of = jnp.sum(jnp.where(chosen, entry[None, None, :], 0), axis=-1)
    local_of = jnp.sum(jnp.where(chosen, (listings % passage_rows)[:, None, :], 0), axis=-1)
    source = jnp.arange(owners, dtype=jnp.int32)[:, None]
    query_of = (source * query_rows + entry_of // listed).reshape(-1)
    local_of = local_of.reshape(-1)
    first = valid & ((entry_of % listed).reshape(-1) == 0)

    smem = pl.BlockSpec(memory_space=pltpu.SMEM)
    vmem = pl.BlockSpec(memory_space=pltpu.VMEM)
    params = pltpu.CompilerParams(vmem_limit_bytes=VMEM_LIMIT)
    block_shape = (passage_rows, psg_len, emb_dim)
    passage_emb, weights, slot_scores = pl.pallas_call(
        score_kernel,
        out_shape=(
            jax.ShapeDtypeStruct(block_shape, jnp.bfloat16),
            jax.ShapeDtypeStruct((slot_total, qry_len, psg_len), f32),
            jax.ShapeDtypeStruct((slot_total, 1, 128), f32),
        ),
        in_specs=[smem, smem, vmem, vmem],
        out_specs=(vmem, vmem, vmem),
        compiler_params=params,
    )(local_of, query_of, passage_pre, visitors)
    slot_scores = slot_scores[:, 0, 0]

    mine = valid[None, :] & (query_of[None, :] == jnp.arange(queries, dtype=jnp.int32)[:, None])
    slot_expo = jnp.exp(slot_scores)
    part_total = jnp.sum(jnp.where(mine, slot_expo[None, :], 0.0), axis=1)
    part_first = jnp.sum(jnp.where(mine & first[None, :], slot_scores[None, :], 0.0), axis=1)
    sums = jnp.sum(spread(jnp.stack([part_total, part_first]), both, owners).reshape(owners, 2, queries), axis=0)
    total_of = jnp.sum(jnp.where(mine, sums[0][:, None], 0.0), axis=0)
    slot_grad = jnp.where(
        valid, slot_expo / jnp.where(valid, total_of, 1.0) - first.astype(f32), 0.0
    )
    losses = lax.dynamic_slice_in_dim(jnp.log(sums[0]) - sums[1], me * query_rows, query_rows)

    query_terms, passage_pre_grad = pl.pallas_call(
        grad_kernel,
        out_shape=(
            jax.ShapeDtypeStruct((queries, qry_len, emb_dim), jnp.bfloat16),
            jax.ShapeDtypeStruct(block_shape, jnp.bfloat16),
        ),
        in_specs=[smem, smem, smem, vmem, vmem, vmem, vmem],
        out_specs=(vmem, vmem),
        scratch_shapes=[
            pltpu.VMEM((queries, qry_len, emb_dim), f32),
            pltpu.VMEM(block_shape, f32),
        ],
        compiler_params=params,
    )(local_of, query_of, slot_grad, passage_pre, passage_emb, visitors, weights)

    terms_back = exchange(query_terms.reshape(owners, query_rows, qry_len, emb_dim), both)
    query_emb_grad = jnp.sum(
        terms_back.reshape(owners, query_rows, qry_len, emb_dim).astype(f32), axis=0
    )
    query_pre_grad = unit_back(query_emb_grad, query_unit, query_norm)
    passage_all = gather_mp(passage_pre_grad, groups)
    query_all = gather_mp(query_pre_grad, groups)
    weight_part = jnp.einsum("nlh,nle->he", query_states, query_all, preferred_element_type=f32)
    weight_part = weight_part + jnp.einsum(
        "nhl,nle->he", passage_states, passage_all, preferred_element_type=f32
    )
    height = weight_part.shape[0] // replicas
    pieces = exchange(weight_part.reshape(replicas, height, emb_dim), "dp")
    piece = jnp.sum(pieces.reshape(replicas, height, emb_dim), axis=0)
    weight_grad = spread(piece, "dp", replicas).reshape(weight_part.shape)
    query_grads = jnp.einsum("nle,he->nlh", query_all, projection, preferred_element_type=f32)
    passage_grads = jnp.einsum("nle,he->nhl", passage_all, projection, preferred_element_type=f32)
    return (losses, weight_grad, query_grads, passage_grads)


def solution(mesh):
    return jax.shard_map(
        on_device,
        mesh=mesh,
        in_specs=(P("dp", None, "mp"), P("dp", "mp", None), P("mp", None), P(("dp", "mp"), None)),
        out_specs=(P(("dp", "mp")), P("mp", None), P("dp", None, "mp"), P("dp", "mp", None)),
        check_vma=False,
    )
```

```python
import jax
import jax.numpy as jnp
from jax import lax
from jax.experimental import pallas as pl
from jax.experimental.pallas import tpu as pltpu
from jax.sharding import PartitionSpec as P

sharpness = 10.0
norm_eps = 1e-06
BATCH = 8
VMEM_LIMIT = 56 * 1024 * 1024


def unit_rows(pre):
    norm = jnp.sqrt(jnp.sum(pre * pre, axis=-1, keepdims=True) + norm_eps)
    return (pre / norm, norm)


def unit_back(grad, unit, norm):
    inner = jnp.sum(grad * unit, axis=-1, keepdims=True)
    return ((grad - unit * inner) / norm).astype(jnp.bfloat16)


def score_kernel(local_ref, query_ref, pre_ref, visitors_ref, emb_ref, weights_ref, scores_ref):
    def embed(p, carry):
        unit, _ = unit_rows(pre_ref[p])
        emb_ref[p] = unit.astype(jnp.bfloat16)
        return carry

    lax.fori_loop(0, pre_ref.shape[0], embed, 0)

    def slots(b, carry):
        first = b * BATCH
        sims = [
            lax.dot_general(
                visitors_ref[query_ref[first + u]],
                emb_ref[local_ref[first + u]],
                (((1,), (1,)), ((), ())),
                preferred_element_type=jnp.float32,
            )
            for u in range(BATCH)
        ]
        expos = [jnp.exp(sharpness * sim) for sim in sims]
        totals = [jnp.sum(expo, axis=-1, keepdims=True) for expo in expos]
        for u in range(BATCH):
            weights_ref[first + u] = expos[u] / totals[u]
        for u in range(BATCH):
            score = jnp.sum(jnp.log(totals[u]), axis=0, keepdims=True) / sharpness
            scores_ref[first + u] = jnp.broadcast_to(score, scores_ref.shape[1:])
        return carry

    lax.fori_loop(0, weights_ref.shape[0] // BATCH, slots, 0)


def slot_grad_of(grad_ref, weights_ref, s):
    return (grad_ref[s] * weights_ref[s]).astype(jnp.bfloat16)


def passage_kernel(
    local_ref, query_ref, grad_ref, pre_ref, visitors_ref, weights_ref, pre_grad_ref, passage_sum
):
    passage_sum[...] = jnp.zeros_like(passage_sum)

    def slots(b, carry):
        first = b * BATCH
        terms = [
            lax.dot_general(
                slot_grad_of(grad_ref, weights_ref, first + u),
                visitors_ref[query_ref[first + u]],
                (((0,), (0,)), ((), ())),
                preferred_element_type=jnp.float32,
            )
            for u in range(BATCH)
        ]
        for u in range(BATCH):
            passage_sum[local_ref[first + u]] += terms[u]
        return carry

    lax.fori_loop(0, weights_ref.shape[0] // BATCH, slots, 0)

    def back(p, carry):
        unit, norm = unit_rows(pre_ref[p])
        pre_grad_ref[p] = unit_back(passage_sum[p], unit, norm)
        return carry

    lax.fori_loop(0, pre_ref.shape[0], back, 0)


def query_kernel(
    local_ref, query_ref, grad_ref, emb_ref, weights_ref, query_grad_ref, query_sum
):
    query_sum[...] = jnp.zeros_like(query_sum)

    def slots(b, carry):
        first = b * BATCH
        terms = [
            jnp.dot(
                slot_grad_of(grad_ref, weights_ref, first + u),
                emb_ref[local_ref[first + u]],
                preferred_element_type=jnp.float32,
            )
            for u in range(BATCH)
        ]
        for u in range(BATCH):
            query_sum[query_ref[first + u]] += terms[u]
        return carry

    lax.fori_loop(0, weights_ref.shape[0] // BATCH, slots, 0)
    query_grad_ref[...] = query_sum[...].astype(jnp.bfloat16)


def swap(array, bit, groups):
    return lax.ppermute(array, "mp", [(i, i ^ bit) for i in range(groups)])


def reduce_mp(states, project, groups, dtype, later=()):
    f32 = jnp.float32
    me = lax.axis_index("mp")
    rows = states.shape[0] // groups

    def block(index):
        return project(lax.dynamic_slice_in_dim(states, index * rows, rows, 0))

    if groups != 4:
        whole = lax.psum_scatter(project(states), "mp", scatter_dimension=0, tiled=True)
        return whole, later
    far_out = swap(block(me ^ 3).astype(dtype), 1, groups)
    near_out = swap(block(me ^ 1).astype(dtype), 1, groups)
    far = (block(me ^ 2) + far_out.astype(f32)).astype(dtype)
    far, later = lax.optimization_barrier((far, later))
    far_in = swap(far, 2, groups)
    return (block(me) + near_out.astype(f32)) + far_in.astype(f32), later


def gather_mp(mine, groups):
    if groups != 4:
        return lax.all_gather(mine, "mp", axis=0, tiled=True)
    me = lax.axis_index("mp")
    far = swap(mine, 2, groups)
    near = swap(mine, 1, groups)
    far_near = swap(far, 1, groups)
    odd = (me & 1) == 1
    here = jnp.concatenate([jnp.where(odd, near, mine), jnp.where(odd, mine, near)])
    there = jnp.concatenate([jnp.where(odd, far_near, far), jnp.where(odd, far, far_near)])
    high = (me & 2) == 2
    return jnp.concatenate([jnp.where(high, there, here), jnp.where(high, here, there)])


def exchange(array, axes):
    return lax.all_to_all(array, axes, split_axis=0, concat_axis=0, tiled=True)


def spread(array, axes, size):
    return exchange(jnp.broadcast_to(array[None], (size,) + array.shape), axes)


def on_device(query_states, passage_states, projection, candidates):
    f32 = jnp.float32
    both = ("dp", "mp")
    owners = lax.axis_size(both)
    groups = lax.axis_size("mp")
    replicas = lax.axis_size("dp")
    me = lax.axis_index(both)
    query_rows, listed = candidates.shape
    qry_len = query_states.shape[1]
    emb_dim = projection.shape[1]
    psg_len = passage_states.shape[2]
    passage_rows = passage_states.shape[0] // groups
    requests = query_rows * listed
    capacity = 2 * requests // owners
    slot_total = owners * capacity
    queries = owners * query_rows

    passage_pre, (query_late, candidates_late) = reduce_mp(
        passage_states,
        lambda s: jnp.einsum("nhl,he->nle", s, projection, preferred_element_type=f32),
        groups,
        jnp.bfloat16,
        (query_states, candidates),
    )
    query_pre, _ = reduce_mp(
        query_late,
        lambda s: jnp.einsum("nlh,he->nle", s, projection, preferred_element_type=f32),
        groups,
        f32,
    )
    listings = spread(candidates_late, both, owners).reshape(owners, requests)
    query_unit, query_norm = unit_rows(query_pre)
    visitors = spread(query_unit.astype(jnp.bfloat16), both, owners)
    visitors = visitors.reshape(queries, qry_len, emb_dim)

    held = (listings // passage_rows) == me
    within = jnp.cumsum(held.astype(jnp.int32), axis=1) - 1
    chosen = held[:, None, :] & (
        within[:, None, :] == jnp.arange(capacity, dtype=jnp.int32)[None, :, None]
    )
    entry = jnp.arange(requests, dtype=jnp.int32)
    valid = jnp.any(chosen, axis=-1).reshape(-1)
    entry_of = jnp.sum(jnp.where(chosen, entry[None, None, :], 0), axis=-1)
    local_of = jnp.sum(jnp.where(chosen, (listings % passage_rows)[:, None, :], 0), axis=-1)
    source = jnp.arange(owners, dtype=jnp.int32)[:, None]
    query_of = (source * query_rows + entry_of // listed).reshape(-1)
    local_of = local_of.reshape(-1)
    first = valid & ((entry_of % listed).reshape(-1) == 0)

    smem = pl.BlockSpec(memory_space=pltpu.SMEM)
    vmem = pl.BlockSpec(memory_space=pltpu.VMEM)
    params = pltpu.CompilerParams(vmem_limit_bytes=VMEM_LIMIT)
    block_shape = (passage_rows, psg_len, emb_dim)
    passage_emb, weights, slot_scores = pl.pallas_call(
        score_kernel,
        out_shape=(
            jax.ShapeDtypeStruct(block_shape, jnp.bfloat16),
            jax.ShapeDtypeStruct((slot_total, qry_len, psg_len), f32),
            jax.ShapeDtypeStruct((slot_total, 1, 128), f32),
        ),
        in_specs=[smem, smem, vmem, vmem],
        out_specs=(vmem, vmem, vmem),
        compiler_params=params,
    )(local_of, query_of, passage_pre, visitors)
    slot_scores = slot_scores[:, 0, 0]

    mine = valid[None, :] & (query_of[None, :] == jnp.arange(queries, dtype=jnp.int32)[:, None])
    slot_expo = jnp.exp(slot_scores)
    part_total = jnp.sum(jnp.where(mine, slot_expo[None, :], 0.0), axis=1)
    part_first = jnp.sum(jnp.where(mine & first[None, :], slot_scores[None, :], 0.0), axis=1)
    sums = jnp.sum(spread(jnp.stack([part_total, part_first]), both, owners).reshape(owners, 2, queries), axis=0)
    total_of = jnp.sum(jnp.where(mine, sums[0][:, None], 0.0), axis=0)
    slot_grad = jnp.where(
        valid, slot_expo / jnp.where(valid, total_of, 1.0) - first.astype(f32), 0.0
    )
    losses = lax.dynamic_slice_in_dim(jnp.log(sums[0]) - sums[1], me * query_rows, query_rows)

    passage_pre_grad = pl.pallas_call(
        passage_kernel,
        out_shape=jax.ShapeDtypeStruct(block_shape, jnp.bfloat16),
        in_specs=[smem, smem, smem, vmem, vmem, vmem],
        out_specs=vmem,
        scratch_shapes=[pltpu.VMEM(block_shape, f32)],
        compiler_params=params,
    )(local_of, query_of, slot_grad, passage_pre, visitors, weights)
    passage_pre_grad, slot_grad = lax.optimization_barrier((passage_pre_grad, slot_grad))
    work = slot_total * qry_len * psg_len
    query_terms = pl.pallas_call(
        query_kernel,
        out_shape=jax.ShapeDtypeStruct((queries, qry_len, emb_dim), jnp.bfloat16),
        in_specs=[smem, smem, smem, vmem, vmem],
        out_specs=vmem,
        scratch_shapes=[pltpu.VMEM((queries, qry_len, emb_dim), f32)],
        compiler_params=params,
        cost_estimate=pl.CostEstimate(
            flops=2 * work * emb_dim, bytes_accessed=4 * work, transcendentals=0
        ),
    )(local_of, query_of, slot_grad, passage_emb, weights)

    terms_back = exchange(query_terms.reshape(owners, query_rows, qry_len, emb_dim), both)
    query_emb_grad = jnp.sum(
        terms_back.reshape(owners, query_rows, qry_len, emb_dim).astype(f32), axis=0
    )
    query_pre_grad = unit_back(query_emb_grad, query_unit, query_norm)
    passage_all = gather_mp(passage_pre_grad, groups)
    query_all = gather_mp(query_pre_grad, groups)
    weight_part = jnp.einsum("nlh,nle->he", query_states, query_all, preferred_element_type=f32)
    weight_part = weight_part + jnp.einsum(
        "nhl,nle->he", passage_states, passage_all, preferred_element_type=f32
    )
    shares = spread(weight_part.astype(jnp.bfloat16), "dp", replicas)
    weight_grad = jnp.sum(shares.reshape((replicas,) + weight_part.shape).astype(f32), axis=0)
    query_grads = jnp.einsum("nle,he->nlh", query_all, projection, preferred_element_type=f32)
    passage_grads = jnp.einsum("nle,he->nhl", passage_all, projection, preferred_element_type=f32)
    return (losses, weight_grad, query_grads, passage_grads)


def solution(mesh):
    return jax.shard_map(
        on_device,
        mesh=mesh,
        in_specs=(P("dp", None, "mp"), P("dp", "mp", None), P("mp", None), P(("dp", "mp"), None)),
        out_specs=(P(("dp", "mp")), P("mp", None), P("dp", None, "mp"), P("dp", "mp", None)),
        check_vma=False,
    )
```

```python
import jax
import jax.numpy as jnp
from jax import lax
from jax.experimental import pallas as pl
from jax.experimental.pallas import tpu as pltpu
from jax.sharding import PartitionSpec as P

sharpness = 10.0
norm_eps = 1e-06
BATCH = 8
VMEM_LIMIT = 56 * 1024 * 1024


def unit_rows(pre):
    norm = jnp.sqrt(jnp.sum(pre * pre, axis=-1, keepdims=True) + norm_eps)
    return (pre / norm, norm)


def unit_back(grad, unit, norm):
    inner = jnp.sum(grad * unit, axis=-1, keepdims=True)
    return ((grad - unit * inner) / norm).astype(jnp.bfloat16)


def score_kernel(local_ref, query_ref, pre_ref, visitors_ref, emb_ref, weights_ref, scores_ref):
    def embed(p, carry):
        unit, _ = unit_rows(pre_ref[p])
        emb_ref[p] = unit.astype(jnp.bfloat16)
        return carry

    lax.fori_loop(0, pre_ref.shape[0], embed, 0)

    def slots(b, carry):
        for u in range(BATCH):
            s = b * BATCH + u
            sim = lax.dot_general(
                visitors_ref[query_ref[s]],
                emb_ref[local_ref[s]],
                (((1,), (1,)), ((), ())),
                preferred_element_type=jnp.float32,
            )
            expo = jnp.exp(sharpness * sim)
            total = jnp.sum(expo, axis=-1, keepdims=True)
            weights_ref[s] = expo / total
            score = jnp.sum(jnp.log(total), axis=0, keepdims=True) / sharpness
            scores_ref[s] = jnp.broadcast_to(score, scores_ref.shape[1:])
        return carry

    lax.fori_loop(0, weights_ref.shape[0] // BATCH, slots, 0)


def grad_kernel(
    local_ref, query_ref, grad_ref, pre_ref, emb_ref, visitors_ref, weights_ref,
    query_grad_ref, pre_grad_ref, query_sum, passage_sum
):
    query_sum[...] = jnp.zeros_like(query_sum)
    passage_sum[...] = jnp.zeros_like(passage_sum)

    def slots(b, carry):
        found = []
        for u in range(BATCH):
            s = b * BATCH + u
            p = local_ref[s]
            q = query_ref[s]
            sim_grad = (grad_ref[s] * weights_ref[s]).astype(jnp.bfloat16)
            query_term = jnp.dot(sim_grad, emb_ref[p], preferred_element_type=jnp.float32)
            passage_term = lax.dot_general(
                sim_grad,
                visitors_ref[q],
                (((0,), (0,)), ((), ())),
                preferred_element_type=jnp.float32,
            )
            found.append((p, q, query_term, passage_term))
        for p, q, query_term, passage_term in found:
            query_sum[q] += query_term
            passage_sum[p] += passage_term
        return carry

    lax.fori_loop(0, weights_ref.shape[0] // BATCH, slots, 0)
    query_grad_ref[...] = query_sum[...].astype(jnp.bfloat16)

    def back(p, carry):
        unit, norm = unit_rows(pre_ref[p])
        pre_grad_ref[p] = unit_back(passage_sum[p], unit, norm)
        return carry

    lax.fori_loop(0, pre_ref.shape[0], back, 0)


def swap(array, bit, groups):
    return lax.ppermute(array, "mp", [(i, i ^ bit) for i in range(groups)])


def reduce_mp(states, project, groups, dtype, later=()):
    f32 = jnp.float32
    me = lax.axis_index("mp")
    rows = states.shape[0] // groups

    def block(index):
        return project(lax.dynamic_slice_in_dim(states, index * rows, rows, 0))

    if groups != 4:
        whole = lax.psum_scatter(project(states), "mp", scatter_dimension=0, tiled=True)
        return whole, later
    far_out = swap(block(me ^ 3).astype(dtype), 1, groups)
    near_out = swap(block(me ^ 1).astype(dtype), 1, groups)
    far = (block(me ^ 2) + far_out.astype(f32)).astype(dtype)
    if later:
        far, later = lax.optimization_barrier((far, later))
    far_in = swap(far, 2, groups)
    return (block(me) + near_out.astype(f32)) + far_in.astype(f32), later


def gather_mp(mine, groups):
    if groups != 4:
        return lax.all_gather(mine, "mp", axis=0, tiled=True)
    me = lax.axis_index("mp")
    far = swap(mine, 2, groups)
    near = swap(mine, 1, groups)
    far_near = swap(far, 1, groups)
    odd = (me & 1) == 1
    here = jnp.concatenate([jnp.where(odd, near, mine), jnp.where(odd, mine, near)])
    there = jnp.concatenate([jnp.where(odd, far_near, far), jnp.where(odd, far, far_near)])
    high = (me & 2) == 2
    return jnp.concatenate([jnp.where(high, there, here), jnp.where(high, here, there)])


def exchange(array, axes):
    return lax.all_to_all(array, axes, split_axis=0, concat_axis=0, tiled=True)


def spread(array, axes, size):
    return exchange(jnp.broadcast_to(array[None], (size,) + array.shape), axes)


def on_device(query_states, passage_states, projection, candidates):
    f32 = jnp.float32
    both = ("dp", "mp")
    owners = lax.axis_size(both)
    groups = lax.axis_size("mp")
    replicas = lax.axis_size("dp")
    me = lax.axis_index(both)
    query_rows, listed = candidates.shape
    qry_len = query_states.shape[1]
    emb_dim = projection.shape[1]
    psg_len = passage_states.shape[2]
    passage_rows = passage_states.shape[0] // groups
    requests = query_rows * listed
    capacity = 2 * requests // owners
    slot_total = owners * capacity
    queries = owners * query_rows

    query_pre, _ = reduce_mp(
        query_states,
        lambda s: jnp.einsum("nlh,he->nle", s, projection, preferred_element_type=f32),
        groups,
        f32,
    )
    query_unit, query_norm = unit_rows(query_pre)
    visitors = spread(query_unit.astype(jnp.bfloat16), both, owners)
    visitors = visitors.reshape(queries, qry_len, emb_dim)
    passage_pre, (candidates_late,) = reduce_mp(
        passage_states,
        lambda s: jnp.einsum("nhl,he->nle", s, projection, preferred_element_type=f32),
        groups,
        jnp.bfloat16,
        (candidates,),
    )
    listings = spread(candidates_late, both, owners).reshape(owners, requests)

    held = (listings // passage_rows) == me
    within = jnp.cumsum(held.astype(jnp.int32), axis=1) - 1
    chosen = held[:, None, :] & (
        within[:, None, :] == jnp.arange(capacity, dtype=jnp.int32)[None, :, None]
    )
    entry = jnp.arange(requests, dtype=jnp.int32)
    valid = jnp.any(chosen, axis=-1).reshape(-1)
    entry_of = jnp.sum(jnp.where(chosen, entry[None, None, :], 0), axis=-1)
    local_of = jnp.sum(jnp.where(chosen, (listings % passage_rows)[:, None, :], 0), axis=-1)
    source = jnp.arange(owners, dtype=jnp.int32)[:, None]
    query_of = (source * query_rows + entry_of // listed).reshape(-1)
    local_of = local_of.reshape(-1)
    first = valid & ((entry_of % listed).reshape(-1) == 0)

    smem = pl.BlockSpec(memory_space=pltpu.SMEM)
    vmem = pl.BlockSpec(memory_space=pltpu.VMEM)
    params = pltpu.CompilerParams(vmem_limit_bytes=VMEM_LIMIT)
    block_shape = (passage_rows, psg_len, emb_dim)
    passage_emb, weights, slot_scores = pl.pallas_call(
        score_kernel,
        out_shape=(
            jax.ShapeDtypeStruct(block_shape, jnp.bfloat16),
            jax.ShapeDtypeStruct((slot_total, qry_len, psg_len), f32),
            jax.ShapeDtypeStruct((slot_total, 1, 128), f32),
        ),
        in_specs=[smem, smem, vmem, vmem],
        out_specs=(vmem, vmem, vmem),
        compiler_params=params,
    )(local_of, query_of, passage_pre, visitors)
    slot_scores = slot_scores[:, 0, 0]

    mine = valid[None, :] & (query_of[None, :] == jnp.arange(queries, dtype=jnp.int32)[:, None])
    slot_expo = jnp.exp(slot_scores)
    part_total = jnp.sum(jnp.where(mine, slot_expo[None, :], 0.0), axis=1)
    part_first = jnp.sum(jnp.where(mine & first[None, :], slot_scores[None, :], 0.0), axis=1)
    sums = jnp.sum(spread(jnp.stack([part_total, part_first]), both, owners).reshape(owners, 2, queries), axis=0)
    total_of = jnp.sum(jnp.where(mine, sums[0][:, None], 0.0), axis=0)
    slot_grad = jnp.where(
        valid, slot_expo / jnp.where(valid, total_of, 1.0) - first.astype(f32), 0.0
    )
    losses = lax.dynamic_slice_in_dim(jnp.log(sums[0]) - sums[1], me * query_rows, query_rows)

    query_terms, passage_pre_grad = pl.pallas_call(
        grad_kernel,
        out_shape=(
            jax.ShapeDtypeStruct((queries, qry_len, emb_dim), jnp.bfloat16),
            jax.ShapeDtypeStruct(block_shape, jnp.bfloat16),
        ),
        in_specs=[smem, smem, smem, vmem, vmem, vmem, vmem],
        out_specs=(vmem, vmem),
        scratch_shapes=[
            pltpu.VMEM((queries, qry_len, emb_dim), f32),
            pltpu.VMEM(block_shape, f32),
        ],
        compiler_params=params,
    )(local_of, query_of, slot_grad, passage_pre, passage_emb, visitors, weights)

    terms_back = exchange(query_terms.reshape(owners, query_rows, qry_len, emb_dim), both)
    query_emb_grad = jnp.sum(
        terms_back.reshape(owners, query_rows, qry_len, emb_dim).astype(f32), axis=0
    )
    query_pre_grad = unit_back(query_emb_grad, query_unit, query_norm)
    passage_all = gather_mp(passage_pre_grad, groups)
    query_all = gather_mp(query_pre_grad, groups)
    weight_part = jnp.einsum("nlh,nle->he", query_states, query_all, preferred_element_type=f32)
    weight_part = weight_part + jnp.einsum(
        "nhl,nle->he", passage_states, passage_all, preferred_element_type=f32
    )
    shares = spread(weight_part.astype(jnp.bfloat16), "dp", replicas)
    weight_grad = jnp.sum(shares.reshape((replicas,) + weight_part.shape).astype(f32), axis=0)
    query_grads = jnp.einsum("nle,he->nlh", query_all, projection, preferred_element_type=f32)
    passage_grads = jnp.einsum("nle,he->nhl", passage_all, projection, preferred_element_type=f32)
    return (losses, weight_grad, query_grads, passage_grads)


def solution(mesh):
    return jax.shard_map(
        on_device,
        mesh=mesh,
        in_specs=(P("dp", None, "mp"), P("dp", "mp", None), P("mp", None), P(("dp", "mp"), None)),
        out_specs=(P(("dp", "mp")), P("mp", None), P("dp", None, "mp"), P("dp", "mp", None)),
        check_vma=False,
    )
```

```python
import functools

import jax
import jax.numpy as jnp
from jax import lax
from jax.experimental import pallas as pl
from jax.experimental.pallas import tpu as pltpu
from jax.sharding import PartitionSpec as P

sharpness = 10.0
norm_eps = 1e-06
BATCH = 8
VMEM_LIMIT = 56 * 1024 * 1024


def unit_rows(pre):
    norm = jnp.sqrt(jnp.sum(pre * pre, axis=-1, keepdims=True) + norm_eps)
    return (pre / norm, norm)


def unit_back(grad, unit, norm):
    inner = jnp.sum(grad * unit, axis=-1, keepdims=True)
    return ((grad - unit * inner) / norm).astype(jnp.bfloat16)


def unit_and_scale(pre):
    scale = lax.rsqrt(jnp.sum(pre * pre, axis=-1, keepdims=True) + norm_eps)
    return (pre * scale, scale)


def score_kernel(local_ref, query_ref, pre_ref, visitors_ref, emb_ref, weights_ref, scores_ref):
    def embed(p, carry):
        unit, _ = unit_and_scale(pre_ref[p])
        emb_ref[p] = unit.astype(jnp.bfloat16)
        return carry

    lax.fori_loop(0, pre_ref.shape[0], embed, 0, unroll=4)

    def slots(b, carry):
        for u in range(BATCH):
            s = b * BATCH + u
            sim = lax.dot_general(
                visitors_ref[query_ref[s]],
                emb_ref[local_ref[s]],
                (((1,), (1,)), ((), ())),
                preferred_element_type=jnp.float32,
            )
            expo = jnp.exp(sharpness * sim)
            total = jnp.sum(expo, axis=-1, keepdims=True)
            weights_ref[s] = expo / total
            parts = [total[8 * i : 8 * i + 8] for i in range(total.shape[0] // 8)]
            logs = [jnp.log(functools.reduce(jnp.multiply, parts[i : i + 4])) for i in range(0, len(parts), 4)]
            score = jnp.sum(functools.reduce(jnp.add, logs), axis=0, keepdims=True) / sharpness
            scores_ref[s] = jnp.broadcast_to(score, scores_ref.shape[1:])
        return carry

    lax.fori_loop(0, weights_ref.shape[0] // BATCH, slots, 0)


def grad_kernel(
    local_ref, query_ref, grad_ref, pre_ref, emb_ref, visitors_ref, weights_ref,
    query_grad_ref, pre_grad_ref, query_sum, passage_sum
):
    query_sum[...] = jnp.zeros_like(query_sum)
    passage_sum[...] = jnp.zeros_like(passage_sum)

    def slots(b, carry):
        found = []
        for u in range(BATCH):
            s = b * BATCH + u
            p = local_ref[s]
            q = query_ref[s]
            sim_grad = (grad_ref[s] * weights_ref[s]).astype(jnp.bfloat16)
            query_term = jnp.dot(sim_grad, emb_ref[p], preferred_element_type=jnp.float32)
            passage_term = lax.dot_general(
                sim_grad,
                visitors_ref[q],
                (((0,), (0,)), ((), ())),
                preferred_element_type=jnp.float32,
            )
            found.append((p, q, query_term, passage_term))
        for p, q, query_term, passage_term in found:
            query_sum[q] += query_term
            passage_sum[p] += passage_term
        return carry

    lax.fori_loop(0, weights_ref.shape[0] // BATCH, slots, 0)
    query_grad_ref[...] = query_sum[...].astype(jnp.bfloat16)

    def back(p, carry):
        unit, scale = unit_and_scale(pre_ref[p])
        grad = passage_sum[p]
        inner = jnp.sum(grad * unit, axis=-1, keepdims=True)
        pre_grad_ref[p] = ((grad - unit * inner) * scale).astype(jnp.bfloat16)
        return carry

    lax.fori_loop(0, pre_ref.shape[0], back, 0, unroll=4)


def swap(array, bit, groups):
    return lax.ppermute(array, "mp", [(i, i ^ bit) for i in range(groups)])


def reduce_mp(states, project, groups, dtype):
    f32 = jnp.float32
    me = lax.axis_index("mp")
    rows = states.shape[0] // groups

    def block(index):
        return project(lax.dynamic_slice_in_dim(states, index * rows, rows, 0))

    if groups != 4:
        return lax.psum_scatter(project(states), "mp", scatter_dimension=0, tiled=True)
    far_out = swap(block(me ^ 3).astype(dtype), 1, groups)
    near_out = swap(block(me ^ 1).astype(dtype), 1, groups)
    far = (block(me ^ 2) + far_out.astype(f32)).astype(dtype)
    far_in = swap(far, 2, groups)
    return (block(me) + near_out.astype(f32)) + far_in.astype(f32)


def gather_mp(mine, groups):
    if groups != 4:
        return lax.all_gather(mine, "mp", axis=0, tiled=True)
    me = lax.axis_index("mp")
    far = swap(mine, 2, groups)
    near = swap(mine, 1, groups)
    far_near = swap(far, 1, groups)
    odd = (me & 1) == 1
    here = jnp.concatenate([jnp.where(odd, near, mine), jnp.where(odd, mine, near)])
    there = jnp.concatenate([jnp.where(odd, far_near, far), jnp.where(odd, far, far_near)])
    high = (me & 2) == 2
    return jnp.concatenate([jnp.where(high, there, here), jnp.where(high, here, there)])


def exchange(array, axes):
    return lax.all_to_all(array, axes, split_axis=0, concat_axis=0, tiled=True)


def spread(array, axes, size):
    return exchange(jnp.broadcast_to(array[None], (size,) + array.shape), axes)


def on_device(query_states, passage_states, projection, candidates):
    f32 = jnp.float32
    both = ("dp", "mp")
    owners = lax.axis_size(both)
    groups = lax.axis_size("mp")
    replicas = lax.axis_size("dp")
    me = lax.axis_index(both)
    query_rows, listed = candidates.shape
    qry_len = query_states.shape[1]
    emb_dim = projection.shape[1]
    psg_len = passage_states.shape[2]
    passage_rows = passage_states.shape[0] // groups
    requests = query_rows * listed
    capacity = 2 * requests // owners
    slot_total = owners * capacity
    queries = owners * query_rows

    query_pre = reduce_mp(
        query_states,
        lambda s: jnp.einsum("nlh,he->nle", s, projection, preferred_element_type=f32),
        groups,
        f32,
    )
    query_unit, query_norm = unit_rows(query_pre)
    id_rows = candidates.reshape(-1, emb_dim)
    token_rows = query_rows * qry_len
    message = jnp.concatenate(
        [query_unit.astype(jnp.bfloat16).reshape(token_rows, emb_dim)]
        + [part.astype(jnp.bfloat16) for part in (id_rows // 256, id_rows % 256)]
    )
    message = spread(message, both, owners).reshape(owners, -1, emb_dim)
    visitors = message[:, :token_rows].reshape(queries, qry_len, emb_dim)
    parts = message[:, token_rows:].astype(f32).astype(jnp.int32)
    parts = parts.reshape(owners, 2, requests)
    listings = parts[:, 0] * 256 + parts[:, 1]
    passage_pre = reduce_mp(
        passage_states,
        lambda s: jnp.einsum("nhl,he->nle", s, projection, preferred_element_type=f32),
        groups,
        jnp.bfloat16,
    )

    held = (listings // passage_rows) == me
    within = jnp.cumsum(held.astype(jnp.int32), axis=1) - 1
    chosen = held[:, None, :] & (
        within[:, None, :] == jnp.arange(capacity, dtype=jnp.int32)[None, :, None]
    )
    entry = jnp.arange(requests, dtype=jnp.int32)
    valid = jnp.any(chosen, axis=-1).reshape(-1)
    entry_of = jnp.sum(jnp.where(chosen, entry[None, None, :], 0), axis=-1)
    local_of = jnp.sum(jnp.where(chosen, (listings % passage_rows)[:, None, :], 0), axis=-1)
    source = jnp.arange(owners, dtype=jnp.int32)[:, None]
    query_of = (source * query_rows + entry_of // listed).reshape(-1)
    local_of = local_of.reshape(-1)
    first = valid & ((entry_of % listed).reshape(-1) == 0)

    smem = pl.BlockSpec(memory_space=pltpu.SMEM)
    vmem = pl.BlockSpec(memory_space=pltpu.VMEM)
    params = pltpu.CompilerParams(vmem_limit_bytes=VMEM_LIMIT)
    block_shape = (passage_rows, psg_len, emb_dim)
    passage_emb, weights, slot_scores = pl.pallas_call(
        score_kernel,
        out_shape=(
            jax.ShapeDtypeStruct(block_shape, jnp.bfloat16),
            jax.ShapeDtypeStruct((slot_total, qry_len, psg_len), f32),
            jax.ShapeDtypeStruct((slot_total, 1, 128), f32),
        ),
        in_specs=[smem, smem, vmem, vmem],
        out_specs=(vmem, vmem, vmem),
        compiler_params=params,
    )(local_of, query_of, passage_pre, visitors)
    slot_scores = slot_scores[:, 0, 0]

    mine = valid[None, :] & (query_of[None, :] == jnp.arange(queries, dtype=jnp.int32)[:, None])
    slot_expo = jnp.exp(slot_scores)
    part_total = jnp.sum(jnp.where(mine, slot_expo[None, :], 0.0), axis=1)
    part_first = jnp.sum(jnp.where(mine & first[None, :], slot_scores[None, :], 0.0), axis=1)
    sums = jnp.sum(spread(jnp.stack([part_total, part_first]), both, owners).reshape(owners, 2, queries), axis=0)
    total_of = jnp.sum(jnp.where(mine, sums[0][:, None], 0.0), axis=0)
    slot_grad = jnp.where(
        valid, slot_expo / jnp.where(valid, total_of, 1.0) - first.astype(f32), 0.0
    )
    losses = lax.dynamic_slice_in_dim(jnp.log(sums[0]) - sums[1], me * query_rows, query_rows)

    query_terms, passage_pre_grad = pl.pallas_call(
        grad_kernel,
        out_shape=(
            jax.ShapeDtypeStruct((queries, qry_len, emb_dim), jnp.bfloat16),
            jax.ShapeDtypeStruct(block_shape, jnp.bfloat16),
        ),
        in_specs=[smem, smem, smem, vmem, vmem, vmem, vmem],
        out_specs=(vmem, vmem),
        scratch_shapes=[
            pltpu.VMEM((queries, qry_len, emb_dim), f32),
            pltpu.VMEM(block_shape, f32),
        ],
        compiler_params=params,
    )(local_of, query_of, slot_grad, passage_pre, passage_emb, visitors, weights)

    terms_back = exchange(query_terms.reshape(owners, query_rows, qry_len, emb_dim), both)
    query_emb_grad = jnp.sum(
        terms_back.reshape(owners, query_rows, qry_len, emb_dim).astype(f32), axis=0
    )
    query_pre_grad = unit_back(query_emb_grad, query_unit, query_norm)
    passage_all = gather_mp(passage_pre_grad, groups)
    query_all = gather_mp(query_pre_grad, groups)
    weight_part = jnp.einsum("nlh,nle->he", query_states, query_all, preferred_element_type=f32)
    weight_part = weight_part + jnp.einsum(
        "nhl,nle->he", passage_states, passage_all, preferred_element_type=f32
    )
    shares = spread(weight_part.astype(jnp.bfloat16), "dp", replicas)
    weight_grad = jnp.sum(shares.reshape((replicas,) + weight_part.shape).astype(f32), axis=0)
    query_grads = jnp.einsum("nle,he->nlh", query_all, projection, preferred_element_type=f32)
    passage_grads = jnp.einsum("nle,he->nhl", passage_all, projection, preferred_element_type=f32)
    return (losses, weight_grad, query_grads, passage_grads)


def solution(mesh):
    return jax.shard_map(
        on_device,
        mesh=mesh,
        in_specs=(P("dp", None, "mp"), P("dp", "mp", None), P("mp", None), P(("dp", "mp"), None)),
        out_specs=(P(("dp", "mp")), P("mp", None), P("dp", None, "mp"), P("dp", "mp", None)),
        check_vma=False,
    )
```

```python
import functools

import jax
import jax.numpy as jnp
from jax import lax
from jax.experimental import pallas as pl
from jax.experimental.pallas import tpu as pltpu
from jax.sharding import PartitionSpec as P

sharpness = 10.0
norm_eps = 1e-06
BATCH = 8
VMEM_LIMIT = 56 * 1024 * 1024


def unit_rows(pre):
    norm = jnp.sqrt(jnp.sum(pre * pre, axis=-1, keepdims=True) + norm_eps)
    return (pre / norm, norm)


def unit_back(grad, unit, norm):
    inner = jnp.sum(grad * unit, axis=-1, keepdims=True)
    return ((grad - unit * inner) / norm).astype(jnp.bfloat16)


def unit_and_scale(pre):
    scale = lax.rsqrt(jnp.sum(pre * pre, axis=-1, keepdims=True) + norm_eps)
    return (pre * scale, scale)


def score_kernel(local_ref, query_ref, pre_ref, visitors_ref, emb_ref, weights_ref, scores_ref):
    def embed(p, carry):
        unit, _ = unit_and_scale(pre_ref[p])
        emb_ref[p] = unit.astype(jnp.bfloat16)
        return carry

    lax.fori_loop(0, pre_ref.shape[0], embed, 0, unroll=4)

    def slots(b, carry):
        for u in range(BATCH):
            s = b * BATCH + u
            sim = lax.dot_general(
                visitors_ref[query_ref[s]],
                emb_ref[local_ref[s]],
                (((1,), (1,)), ((), ())),
                preferred_element_type=jnp.float32,
            )
            expo = jnp.exp(sharpness * sim)
            total = jnp.sum(expo, axis=-1, keepdims=True)
            weights_ref[s] = expo / total
            parts = [total[8 * i : 8 * i + 8] for i in range(total.shape[0] // 8)]
            logs = [jnp.log(functools.reduce(jnp.multiply, parts[i : i + 4])) for i in range(0, len(parts), 4)]
            score = jnp.sum(functools.reduce(jnp.add, logs), axis=0, keepdims=True) / sharpness
            scores_ref[s] = jnp.broadcast_to(score, scores_ref.shape[1:])
        return carry

    lax.fori_loop(0, weights_ref.shape[0] // BATCH, slots, 0)


def grad_kernel(
    local_ref, query_ref, grad_ref, pre_ref, emb_ref, visitors_ref, weights_ref,
    query_grad_ref, pre_grad_ref, query_sum, passage_sum
):
    query_sum[...] = jnp.zeros_like(query_sum)
    passage_sum[...] = jnp.zeros_like(passage_sum)

    def slots(b, carry):
        found = []
        for u in range(BATCH):
            s = b * BATCH + u
            p = local_ref[s]
            q = query_ref[s]
            sim_grad = (grad_ref[s] * weights_ref[s]).astype(jnp.bfloat16)
            query_term = jnp.dot(sim_grad, emb_ref[p], preferred_element_type=jnp.float32)
            passage_term = lax.dot_general(
                sim_grad,
                visitors_ref[q],
                (((0,), (0,)), ((), ())),
                preferred_element_type=jnp.float32,
            )
            found.append((p, q, query_term, passage_term))
        for p, q, query_term, passage_term in found:
            query_sum[q] += query_term
            passage_sum[p] += passage_term
        return carry

    lax.fori_loop(0, weights_ref.shape[0] // BATCH, slots, 0)
    query_grad_ref[...] = query_sum[...].astype(jnp.bfloat16)

    def back(p, carry):
        unit, scale = unit_and_scale(pre_ref[p])
        grad = passage_sum[p]
        inner = jnp.sum(grad * unit, axis=-1, keepdims=True)
        pre_grad_ref[p] = ((grad - unit * inner) * scale).astype(jnp.bfloat16)
        return carry

    lax.fori_loop(0, pre_ref.shape[0], back, 0, unroll=4)


def swap(array, bit, groups):
    return lax.ppermute(array, "mp", [(i, i ^ bit) for i in range(groups)])


def reduce_mp(states, project, groups, dtype, later=None):
    f32 = jnp.float32
    me = lax.axis_index("mp")
    rows = states.shape[0] // groups

    def block(index):
        return project(lax.dynamic_slice_in_dim(states, index * rows, rows, 0))

    if groups != 4:
        whole = lax.psum_scatter(project(states), "mp", scatter_dimension=0, tiled=True)
        return whole, later
    far_out = swap(block(me ^ 3).astype(dtype), 1, groups)
    near_out = swap(block(me ^ 1).astype(dtype), 1, groups)
    far = (block(me ^ 2) + far_out.astype(f32)).astype(dtype)
    far_in = swap(far, 2, groups)
    near = block(me) + near_out.astype(f32)
    if later is not None:
        near, later = lax.optimization_barrier((near, later))
    return near + far_in.astype(f32), later


def gather_mp(mine, groups):
    if groups != 4:
        return lax.all_gather(mine, "mp", axis=0, tiled=True)
    me = lax.axis_index("mp")
    far = swap(mine, 2, groups)
    near = swap(mine, 1, groups)
    far_near = swap(far, 1, groups)
    odd = (me & 1) == 1
    here = jnp.concatenate([jnp.where(odd, near, mine), jnp.where(odd, mine, near)])
    there = jnp.concatenate([jnp.where(odd, far_near, far), jnp.where(odd, far, far_near)])
    high = (me & 2) == 2
    return jnp.concatenate([jnp.where(high, there, here), jnp.where(high, here, there)])


def exchange(array, axes):
    return lax.all_to_all(array, axes, split_axis=0, concat_axis=0, tiled=True)


def spread(array, axes, size):
    return exchange(jnp.broadcast_to(array[None], (size,) + array.shape), axes)


def on_device(query_states, passage_states, projection, candidates):
    f32 = jnp.float32
    both = ("dp", "mp")
    owners = lax.axis_size(both)
    groups = lax.axis_size("mp")
    replicas = lax.axis_size("dp")
    me = lax.axis_index(both)
    query_rows, listed = candidates.shape
    qry_len = query_states.shape[1]
    emb_dim = projection.shape[1]
    psg_len = passage_states.shape[2]
    passage_rows = passage_states.shape[0] // groups
    requests = query_rows * listed
    capacity = 2 * requests // owners
    slot_total = owners * capacity
    queries = owners * query_rows

    query_pre, _ = reduce_mp(
        query_states,
        lambda s: jnp.einsum("nlh,he->nle", s, projection, preferred_element_type=f32),
        groups,
        f32,
    )
    query_unit, query_norm = unit_rows(query_pre)
    id_rows = candidates.reshape(-1, emb_dim)
    token_rows = query_rows * qry_len
    message = jnp.concatenate(
        [query_unit.astype(jnp.bfloat16).reshape(token_rows, emb_dim)]
        + [part.astype(jnp.bfloat16) for part in (id_rows // 256, id_rows % 256)]
    )
    passage_pre, message = reduce_mp(
        passage_states,
        lambda s: jnp.einsum("nhl,he->nle", s, projection, preferred_element_type=f32),
        groups,
        jnp.bfloat16,
        message,
    )
    message = spread(message, both, owners).reshape(owners, -1, emb_dim)
    visitors = message[:, :token_rows].reshape(queries, qry_len, emb_dim)
    parts = message[:, token_rows:].astype(f32).astype(jnp.int32)
    parts = parts.reshape(owners, 2, requests)
    listings = parts[:, 0] * 256 + parts[:, 1]
    held = (listings // passage_rows) == me
    within = jnp.cumsum(held.astype(jnp.int32), axis=1) - 1
    chosen = held[:, None, :] & (
        within[:, None, :] == jnp.arange(capacity, dtype=jnp.int32)[None, :, None]
    )
    entry = jnp.arange(requests, dtype=jnp.int32)
    valid = jnp.any(chosen, axis=-1).reshape(-1)
    entry_of = jnp.sum(jnp.where(chosen, entry[None, None, :], 0), axis=-1)
    local_of = jnp.sum(jnp.where(chosen, (listings % passage_rows)[:, None, :], 0), axis=-1)
    source = jnp.arange(owners, dtype=jnp.int32)[:, None]
    query_of = (source * query_rows + entry_of // listed).reshape(-1)
    local_of = local_of.reshape(-1)
    first = valid & ((entry_of % listed).reshape(-1) == 0)

    smem = pl.BlockSpec(memory_space=pltpu.SMEM)
    vmem = pl.BlockSpec(memory_space=pltpu.VMEM)
    params = pltpu.CompilerParams(vmem_limit_bytes=VMEM_LIMIT)
    block_shape = (passage_rows, psg_len, emb_dim)
    passage_emb, weights, slot_scores = pl.pallas_call(
        score_kernel,
        out_shape=(
            jax.ShapeDtypeStruct(block_shape, jnp.bfloat16),
            jax.ShapeDtypeStruct((slot_total, qry_len, psg_len), f32),
            jax.ShapeDtypeStruct((slot_total, 1, 128), f32),
        ),
        in_specs=[smem, smem, vmem, vmem],
        out_specs=(vmem, vmem, vmem),
        compiler_params=params,
    )(local_of, query_of, passage_pre, visitors)
    slot_scores = slot_scores[:, 0, 0]

    mine = valid[None, :] & (query_of[None, :] == jnp.arange(queries, dtype=jnp.int32)[:, None])
    slot_expo = jnp.exp(slot_scores)
    part_total = jnp.sum(jnp.where(mine, slot_expo[None, :], 0.0), axis=1)
    part_first = jnp.sum(jnp.where(mine & first[None, :], slot_scores[None, :], 0.0), axis=1)
    sums = jnp.sum(spread(jnp.stack([part_total, part_first]), both, owners).reshape(owners, 2, queries), axis=0)
    total_of = jnp.sum(jnp.where(mine, sums[0][:, None], 0.0), axis=0)
    slot_grad = jnp.where(
        valid, slot_expo / jnp.where(valid, total_of, 1.0) - first.astype(f32), 0.0
    )
    losses = lax.dynamic_slice_in_dim(jnp.log(sums[0]) - sums[1], me * query_rows, query_rows)

    query_terms, passage_pre_grad = pl.pallas_call(
        grad_kernel,
        out_shape=(
            jax.ShapeDtypeStruct((queries, qry_len, emb_dim), jnp.bfloat16),
            jax.ShapeDtypeStruct(block_shape, jnp.bfloat16),
        ),
        in_specs=[smem, smem, smem, vmem, vmem, vmem, vmem],
        out_specs=(vmem, vmem),
        scratch_shapes=[
            pltpu.VMEM((queries, qry_len, emb_dim), f32),
            pltpu.VMEM(block_shape, f32),
        ],
        compiler_params=params,
    )(local_of, query_of, slot_grad, passage_pre, passage_emb, visitors, weights)

    terms_back = exchange(query_terms.reshape(owners, query_rows, qry_len, emb_dim), both)
    query_emb_grad = jnp.sum(
        terms_back.reshape(owners, query_rows, qry_len, emb_dim).astype(f32), axis=0
    )
    query_pre_grad = unit_back(query_emb_grad, query_unit, query_norm)
    passage_all = gather_mp(passage_pre_grad, groups)
    query_all = gather_mp(query_pre_grad, groups)
    weight_part = jnp.einsum("nlh,nle->he", query_states, query_all, preferred_element_type=f32)
    weight_part = weight_part + jnp.einsum(
        "nhl,nle->he", passage_states, passage_all, preferred_element_type=f32
    )
    shares = spread(weight_part.astype(jnp.bfloat16), "dp", replicas)
    weight_grad = jnp.sum(shares.reshape((replicas,) + weight_part.shape).astype(f32), axis=0)
    query_grads = jnp.einsum("nle,he->nlh", query_all, projection, preferred_element_type=f32)
    passage_grads = jnp.einsum("nle,he->nhl", passage_all, projection, preferred_element_type=f32)
    return (losses, weight_grad, query_grads, passage_grads)


def solution(mesh):
    return jax.shard_map(
        on_device,
        mesh=mesh,
        in_specs=(P("dp", None, "mp"), P("dp", "mp", None), P("mp", None), P(("dp", "mp"), None)),
        out_specs=(P(("dp", "mp")), P("mp", None), P("dp", None, "mp"), P("dp", "mp", None)),
        check_vma=False,
    )
```
